32 devices in a mesh: bricks: 32 (over z, y, x, core).
Axes of the slice: x: 2, y: 2, z: 4, core: 2. Of those that a mesh axis runs over, the one named last changes fastest.
Arguments:
- fluid_state: float32 [18, 128, 8, 128], P(None, 'bricks'), as said below
- harmonics: bfloat16 [1681, 128, 8, 128], P(None, 'bricks'), may hold values from -6 to 6
- zone_slot: int32 [128, 8, 128], P('bricks'), may hold values from 0 to 255
- bin_list: int32 [32, 256], P('bricks'), may hold values from 0 to 1023, as said below
- shell_radius: float32 [1024], replicated, as said below
Outputs:
- new_state: float32 [18, 128, 8, 128], P(None, 'bricks')
- potential: float32 [128, 8, 128], P('bricks')
The draws below stay inside these ranges and needn't reach their ends.
Inputs may be any that keep to these rules, and one draw needn't show every extreme that they name: `bin_list`: each row lists 256 distinct bins in rising order. `fluid_state`: density is positive, the x-momentum's magnitude is at most the density, and the densities of two zones beside each other along x differ by a factor of at most 32. `shell_radius`: positive and rising along the bins.
All inputs are finite; a program needn't handle non-finite values.
Results may differ from the reference program's by a relative error of at most 0.00065.
The reference program's roundings to bfloat16 on the way (of `mass` and `shell_field`) count: a program that leaves them out, or rounds other values in their place, can miss the bound.
Values may be sent and summed in bfloat16 or wider, within the bound.
A program may use at most 128 MiB of HBM per device.

```python
import math
import jax
import jax.numpy as jnp
from jax import lax

CX = 4
SPECIES = 13
LMAX = 40
HARM = 1681
NB = 1024
BL = 256
NX = 128
NY = 8
NZ = 128
ZONES = 131072
N_BRICKS = 32


def draw_fluid_state(key, part):
    key = jax.random.fold_in(key, 11)
    keys = jax.random.split(key, 16)
    plane = jnp.arange(NX, dtype=jnp.int32)
    position = (plane.astype(jnp.float32) / max(NX - 1, 1))[:, None, None]
    grid = (NX, NY, NZ)
    heavy_parity = 1
    light_lo, light_hi = (0.2, 0.24)
    heavy_lo, heavy_hi = (4.4, 5.4)
    fast_lo, slow_top = (0.85, 0.3)
    spread_lo, spread_hi = (0.5, 1.5)
    jitter_lo, jitter_hi = (0.6, 1.6)
    floor_lo, floor_hi = (0.15, 0.35)
    heavy = (plane % 2 == heavy_parity)[:, None, None]
    light_rho = jax.random.uniform(keys[0], grid, jnp.float32, light_lo, light_hi)
    heavy_rho = jax.random.uniform(keys[1], grid, jnp.float32, heavy_lo, heavy_hi)
    density = jnp.where(heavy, heavy_rho, light_rho)
    plane_sign = jnp.where(jax.random.randint(keys[2], (NX, 1, 1), 0, 2) == 0, -1.0, 1.0).astype(jnp.float32)
    fast_speed = plane_sign * jax.random.uniform(keys[3], grid, jnp.float32, fast_lo, 1.0)
    slow_speed = jax.random.uniform(keys[4], grid, jnp.float32, -slow_top, slow_top)
    speed = jnp.where(heavy, fast_speed, slow_speed)
    moment_x = density * speed
    moment_y = density * jax.random.uniform(keys[5], grid, jnp.float32, -1.0, 1.0)
    moment_z = density * jax.random.uniform(keys[6], grid, jnp.float32, -1.0, 1.0)
    energy = density * jax.random.uniform(keys[7], grid, jnp.float32, 0.5, 1.0)
    order = jax.random.permutation(keys[9], SPECIES)
    heavy_rich = (order % 2 == 0)[:, None, None, None]
    column = (SPECIES, 1, 1, 1)
    floor = jax.random.uniform(keys[10], column, jnp.float32, floor_lo, floor_hi)
    rich_amp = jax.random.uniform(keys[11], column, jnp.float32, 0.25, 0.5)
    poor_amp = jax.random.uniform(keys[12], column, jnp.float32, 0.05, 0.12)
    slope_sign = jnp.where(jax.random.randint(keys[13], column, 0, 2) == 0, -1.0, 1.0).astype(jnp.float32)
    slope = slope_sign * jax.random.uniform(keys[14], column, jnp.float32, math.log(4.0), math.log(8.0))
    trend = jnp.exp(slope * (position[None] - 0.5))
    jitter = jnp.exp(jax.random.uniform(keys[15], (SPECIES, NX, 1, 1), jnp.float32, math.log(jitter_lo), math.log(jitter_hi)))
    heavy_amp = jnp.where(heavy_rich, rich_amp, poor_amp)
    light_amp = jnp.where(heavy_rich, poor_amp, rich_amp)
    amplitude = jnp.where(heavy[None], heavy_amp, light_amp)
    spread = jax.random.uniform(keys[8], (SPECIES, NX, NY, NZ), jnp.float32, spread_lo, spread_hi)
    fraction = floor + amplitude * trend * jitter * spread
    return jnp.concatenate([density[None], moment_x[None], moment_y[None], moment_z[None], energy[None], density[None] * fraction], axis=0).astype(jnp.float32)


def draw_bin_list(key, part):
    first_key, second_key = jax.random.split(key, 2)
    strides = jax.random.randint(first_key, (N_BRICKS, BL), 1, 4)
    strides = strides.at[:, 0].set(1)
    offsets = jax.random.randint(second_key, (N_BRICKS, 1), 0, NB - 3 * BL + 1)
    row_ids = jnp.arange(N_BRICKS, dtype=jnp.int32)[:, None]
    offsets = jnp.where(row_ids == 0, 0, offsets)
    climbing = jnp.cumsum(strides, axis=1) - 1
    rising = offsets + climbing
    topmost = NB - 1 - jnp.flip(climbing, axis=1)
    return jnp.where(row_ids == N_BRICKS - 1, topmost, rising).astype(jnp.int32)


def draw_shell_radius(key, part):
    jitter = jax.random.uniform(key, (NB,), jnp.float32, 0.0, 1.0)
    positions = jnp.arange(NB, dtype=jnp.float32)
    return (1.0 + 0.25 * (positions + 0.2 + 0.6 * jitter) / NB).astype(jnp.float32)


def plant(array, rng, smallest, high):
    place = [jax.random.randint(jax.random.fold_in(rng, axis), (), 0, length) for axis, length in enumerate(array.shape)]
    longest = array.shape.index(max(array.shape))
    beside = place[:longest] + [(place[longest] + 1) % array.shape[longest]] + place[longest + 1:]
    return array.at[tuple(place)].set(smallest).at[tuple(beside)].set(high)


def steps_of(stream_key, dims, cuts, least, high):
    def one(dim, shards_of):
        steps = jax.random.uniform(jax.random.fold_in(jax.random.fold_in(stream_key, 6), dim), (shards_of,), jnp.float32, least / len(cuts), high / len(cuts))
        return jnp.repeat(jnp.exp(steps), dims[dim] // shards_of).reshape((-1,) + (1,) * (len(dims) - dim - 1))

    level = one(*cuts[0])
    for cut in cuts[1:]:
        level = level * one(*cut)
    return level


def normal_values(stream_key, extent, deviation, limit, cuts=(), kind=jnp.bfloat16):
    gain = steps_of(stream_key, extent, cuts, -0.22, 0.18) if cuts else 1.0
    values = jax.random.normal(stream_key, extent, jnp.float32) * deviation * gain
    return jnp.minimum(jnp.maximum(values, -limit), limit).astype(kind)


def setup_inputs(seed: int = 0) -> dict:
    streams_of = jax.random.split(jax.random.key(seed), 6)
    return {
        "fluid_state": draw_fluid_state(jax.random.fold_in(streams_of[5], 71), 0),
        "harmonics": normal_values(streams_of[1], (HARM, NX, NY, NZ), 1.0, 6.0, ((1, 32),)),
        "zone_slot": plant(jax.random.randint(streams_of[2], (NX, NY, NZ), 0, BL), jax.random.fold_in(streams_of[2], 1), 0, BL - 1).astype(jnp.int32),
        "bin_list": draw_bin_list(jax.random.fold_in(streams_of[5], 71), 0),
        "shell_radius": draw_shell_radius(jax.random.fold_in(streams_of[5], 71), 0),
    }


time_step = 0.05

def chain_link(first_pair, second_pair):
    return (first_pair[0] * second_pair[0], second_pair[0] * first_pair[1] + second_pair[1])

def degrees(harm_count):
    numbers = jnp.arange(harm_count, dtype=jnp.int32)
    marks = jnp.arange(1, LMAX + 1, dtype=jnp.int32) ** 2
    return lax.optimization_barrier(jnp.sum((numbers[:, None] >= marks[None, :]).astype(jnp.int32), axis=1)).astype(jnp.float32)

def log_steps(radius):
    bin_count = radius.shape[0]
    step_in = jnp.concatenate([jnp.zeros((1,), radius.dtype), jnp.log(radius[:-1]) - jnp.log(radius[1:])])
    step_out = jnp.concatenate([step_in[1:], jnp.zeros((1,), radius.dtype)])
    last_row = jnp.arange(bin_count, dtype=jnp.int32) == bin_count - 1
    return (step_in, step_out, last_row)

def shell_terms(moments, radius, degree):
    step_in, step_out, last_row = log_steps(radius)
    scaled = moments / radius[:, None]
    grow_in = jnp.exp((degree[None, :] + 1.0) * step_in[:, None])
    grow_out = jnp.where(last_row[:, None], 0.0, jnp.exp(degree[None, :] * step_out[:, None]))
    inner = lax.associative_scan(chain_link, (grow_in, scaled))[1]
    outer = lax.associative_scan(chain_link, (grow_out, scaled), reverse=True)[1]
    return (inner + outer - scaled).astype(jnp.bfloat16)

def advance(fluid_state, padded, potential_padded, lower_bound, upper_bound):
    channels = fluid_state.shape[0]
    speed = padded[channels]
    fields = padded[:channels]
    face_flux = 0.25 * (speed[1:] + speed[:-1])[None] * (fields[:, 1:] + fields[:, :-1])
    advanced = fluid_state - time_step * (face_flux[:, 1:] - face_flux[:, :-1])
    gradient = 0.5 * (potential_padded[2:] - potential_padded[:-2])
    density = advanced[0]
    momentum = advanced[1] - time_step * fluid_state[0] * gradient
    energy = advanced[4] - time_step * fluid_state[1] * gradient
    fraction = jnp.clip(advanced[5:] / density[None], lower_bound[:, None, None, None], upper_bound[:, None, None, None])
    return jnp.concatenate([density[None], momentum[None], advanced[2:4], energy[None], density[None] * fraction], axis=0)

def reference(fluid_state, harmonics, zone_slot, bin_list, shell_radius):
    channels, full_x, full_y, full_z = fluid_state.shape
    harm_count = harmonics.shape[0]
    slab_zones = CX * full_y * full_z
    degree = degrees(harm_count)
    mass = fluid_state[0].astype(jnp.bfloat16)

    def slab_parts(slab_index):
        first_plane = (slab_index * CX).astype(jnp.int32)
        harm_slab = lax.dynamic_slice_in_dim(harmonics, first_plane, CX, 1).reshape(harm_count, slab_zones).astype(jnp.float32)
        mass_slab = lax.dynamic_slice_in_dim(mass, first_plane, CX, 0).reshape(slab_zones).astype(jnp.float32)
        slot_slab = lax.dynamic_slice_in_dim(zone_slot, first_plane, CX, 0).reshape(slab_zones)
        slab_bins = lax.dynamic_index_in_dim(bin_list, slab_index.astype(jnp.int32), 0, keepdims=False)
        return (harm_slab, mass_slab, slab_bins[slot_slab].astype(jnp.int32))

    def add_slab(slab_index, running):
        harm_slab, mass_slab, zone_bins = slab_parts(jnp.asarray(slab_index, jnp.int32))
        return running + jax.ops.segment_sum(harm_slab.T * mass_slab[:, None], zone_bins, num_segments=NB)
    moments = lax.fori_loop(0, N_BRICKS, add_slab, jnp.zeros((NB, harm_count), jnp.float32))
    shell_field = shell_terms(moments, shell_radius, degree)
    factor = -1.0 / math.sqrt(float(HARM * ZONES))

    def slab_field(slab_index):
        harm_slab, mass_slab, zone_bins = slab_parts(slab_index)
        row_values = shell_field[zone_bins].astype(jnp.float32)
        return (lax.optimization_barrier(jnp.sum(harm_slab.T * row_values, axis=1)) * factor).reshape(CX, full_y, full_z)
    potential = lax.map(slab_field, jnp.arange(N_BRICKS, dtype=jnp.int32)).reshape(full_x, full_y, full_z)
    velocity = fluid_state[1] / fluid_state[0]
    fractions = fluid_state[5:] / fluid_state[0][None]
    lower_bound = lax.optimization_barrier(jnp.min(fractions, axis=(1, 2, 3)))
    upper_bound = lax.optimization_barrier(jnp.max(fractions, axis=(1, 2, 3)))
    extended = jnp.concatenate([fluid_state, velocity[None]], axis=0)
    padded = jnp.pad(extended, ((0, 0), (1, 1), (0, 0), (0, 0)))
    potential_padded = jnp.pad(potential, ((1, 1), (0, 0), (0, 0)))
    new_state = advance(fluid_state, padded, potential_padded, lower_bound, upper_bound)
    return (new_state, potential)
```

```python
import functools
import math

import jax
import jax.numpy as jnp
from jax import lax
from jax.experimental import pallas as pl
from jax.experimental.pallas import tpu as pltpu
from jax.sharding import PartitionSpec as P

LMAX = 40
HARM = 1681
NB = 1024


MESH = pl.DeviceIdType.MESH

time_step = 0.05


def padded_2(cells, sides, width):
    for axis, dim in sides:
        count = lax.axis_size(axis)
        ends = count - 1
        head = lax.slice_in_dim(cells, 0, width, axis=dim)
        tail = lax.slice_in_dim(cells, cells.shape[dim] - width, cells.shape[dim], axis=dim)
        cells = jnp.concatenate(
            [
                lax.ppermute(tail, axis, [(i, (i + 1) % count) for i in range(ends)]),
                cells,
                lax.ppermute(head, axis, [((i + 1) % count, i) for i in range(ends)]),
            ],
            axis=dim,
        )
    return cells


def degrees(harm_count):
    numbers = jnp.arange(harm_count, dtype=jnp.int32)
    marks = jnp.arange(1, LMAX + 1, dtype=jnp.int32) ** 2
    return jnp.sum((numbers[:, None] >= marks[None, :]).astype(jnp.int32), axis=1).astype(
        jnp.float32
    )


def log_steps(radius):
    bin_count = radius.shape[0]
    step_in = jnp.concatenate(
        [jnp.zeros((1,), radius.dtype), jnp.log(radius[:-1]) - jnp.log(radius[1:])]
    )
    step_out = jnp.concatenate([step_in[1:], jnp.zeros((1,), radius.dtype)])
    last_row = jnp.arange(bin_count, dtype=jnp.int32) == bin_count - 1
    return (step_in, step_out, last_row)


def round_up(value, step):
    return -(-value // step) * step


def one_hot(bin_row, row_total, listed):
    rows = lax.broadcasted_iota(jnp.int32, (row_total, listed), 0)
    return jnp.where(rows == bin_row, 1.0, 0.0).astype(jnp.bfloat16)


def exchange_kernel(
    n, group, part_ref, small_ref, grow_in_ref, grow_out_ref, radius_ref,
    shell_ref, extreme_ref,
    got, smalls, total, shell_t, sent_back, came_back,
    small_send, small_recv, part_send, part_recv, back_send, back_recv,
):
    me = lax.axis_index("bricks")
    block = part_ref.shape[1]
    listed = part_ref.shape[2]
    rows = radius_ref.shape[0]
    back_rows = sent_back.shape[1]

    def peer(offset):
        return lax.rem(me + offset, n)

    def source(offset):
        return lax.rem(me - offset + n, n)

    barrier = pltpu.get_barrier_semaphore()

    def greet(offset, carry):
        pl.semaphore_signal(barrier, inc=1, device_id=(peer(offset),), device_id_type=MESH)
        return carry

    lax.fori_loop(1, n, greet, 0)
    smalls[me] = small_ref[...]
    got[me] = part_ref[me]
    total[...] = jnp.zeros_like(total)
    pl.semaphore_wait(barrier, n - 1)

    def small_copy(target, slot):
        return pltpu.make_async_remote_copy(
            src_ref=small_ref, dst_ref=smalls.at[slot], send_sem=small_send.at[target],
            recv_sem=small_recv.at[slot], device_id=(target,), device_id_type=MESH)

    def part_copy(target, slot):
        return pltpu.make_async_remote_copy(
            src_ref=part_ref.at[target], dst_ref=got.at[slot], send_sem=part_send.at[target],
            recv_sem=part_recv.at[slot], device_id=(target,), device_id_type=MESH)

    def back_copy(target, slot):
        return pltpu.make_async_remote_copy(
            src_ref=sent_back.at[target], dst_ref=came_back.at[slot], send_sem=back_send.at[target],
            recv_sem=back_recv.at[slot], device_id=(target,), device_id_type=MESH)

    def send_parts(offset, carry):
        small_copy(peer(offset), me).start()
        part_copy(peer(offset), me).start()
        return carry

    lax.fori_loop(1, n, send_parts, 0)

    def arrive(offset):
        small_copy(peer(offset), source(offset)).wait_recv()
        part_copy(peer(offset), source(offset)).wait_recv()

    def add_group(number, carry):
        for member in range(group):
            offset = number * group + member

            @pl.when(offset > 0)
            def _():
                arrive(offset)

        marks, halves = [], []
        for member in range(group):
            origin = source(number * group + member)
            marks.append(one_hot(smalls[origin, 0:1, :].astype(jnp.int32), rows, listed))
            values = got[origin]
            high = values.astype(jnp.bfloat16).astype(jnp.float32)
            gap = jnp.zeros((64 - block, listed), jnp.float32)
            halves.append(
                jnp.concatenate([high, gap, values - high, gap], axis=0).astype(jnp.bfloat16)
            )
        total[...] += lax.dot_general(
            jnp.concatenate(marks, axis=1), jnp.concatenate(halves, axis=1),
            (((1,), (1,)), ((), ())), preferred_element_type=jnp.float32)
        return carry

    lax.fori_loop(0, n // group, add_group, 0)
    extreme_ref[...] = jnp.max(smalls[...], axis=0)
    both = total[...]
    scaled = (both + pltpu.roll(both, 64, 1)) / radius_ref[...]
    field = -scaled
    for grow_ref, backward in ((grow_in_ref, False), (grow_out_ref, True)):
        factor, value = grow_ref[...], scaled
        step = 1
        while step < rows:
            turn = rows - step if backward else step
            value = value + factor * pltpu.roll(value, turn, 0)
            factor = factor * pltpu.roll(factor, turn, 0)
            step *= 2
        field = field + value
    shell_t[...] = field.T.astype(jnp.bfloat16)

    def select(target):
        marks = one_hot(smalls[target, 0:1, :].astype(jnp.int32), rows, listed)
        return jnp.dot(
            shell_t[0:back_rows, :], marks, preferred_element_type=jnp.float32
        ).astype(jnp.bfloat16)

    def send_back(offset, carry):
        target = peer(offset)
        sent_back[target] = select(target)
        back_copy(target, me).start()
        return carry

    lax.fori_loop(1, n, send_back, 0)
    shell_ref[me] = select(me)

    def finish(offset, carry):
        small_copy(peer(offset), me).wait_send()
        part_copy(peer(offset), me).wait_send()
        back_copy(peer(offset), me).wait_send()
        origin = source(offset)
        back_copy(peer(offset), origin).wait_recv()
        shell_ref[origin] = came_back[origin]
        return carry

    lax.fori_loop(1, n, finish, 0)


def exchange(parts, small, grow_in, grow_out, radius):
    n, block, listed = parts.shape
    rows = radius.shape[0]
    back_rows = round_up(block, 16)
    whole = pl.BlockSpec(memory_space=pltpu.VMEM)
    return pl.pallas_call(
        functools.partial(exchange_kernel, n, 4),
        out_shape=(
            jax.ShapeDtypeStruct((n, back_rows, listed), jnp.bfloat16),
            jax.ShapeDtypeStruct(small.shape, jnp.float32),
        ),
        in_specs=[whole] * 5,
        out_specs=(whole, whole),
        scratch_shapes=[
            pltpu.VMEM((n, block, listed), jnp.float32),
            pltpu.VMEM((n,) + small.shape, jnp.float32),
            pltpu.VMEM((rows, 128), jnp.float32),
            pltpu.VMEM((128, rows), jnp.bfloat16),
            pltpu.VMEM((n, back_rows, listed), jnp.bfloat16),
            pltpu.VMEM((n, back_rows, listed), jnp.bfloat16),
        ] + [pltpu.SemaphoreType.DMA((n,))] * 6,
        compiler_params=pltpu.CompilerParams(
            collective_id=0, has_side_effects=True, vmem_limit_bytes=48 * 1024 * 1024
        ),
    )(parts, small, grow_in, grow_out, radius)


def advance(fluid_state, padded, potential_padded, lower_bound, upper_bound):
    channels = fluid_state.shape[0]
    speed = padded[channels]
    fields = padded[:channels]
    face_flux = 0.25 * (speed[1:] + speed[:-1])[None] * (fields[:, 1:] + fields[:, :-1])
    advanced = fluid_state - time_step * (face_flux[:, 1:] - face_flux[:, :-1])
    gradient = 0.5 * (potential_padded[2:] - potential_padded[:-2])
    density = advanced[0]
    momentum = advanced[1] - time_step * fluid_state[0] * gradient
    energy = advanced[4] - time_step * fluid_state[1] * gradient
    fraction = jnp.clip(
        advanced[5:] / density[None],
        lower_bound[:, None, None, None],
        upper_bound[:, None, None, None],
    )
    return jnp.concatenate(
        [density[None], momentum[None], advanced[2:4], energy[None], density[None] * fraction],
        axis=0,
    )


def per_device(fluid_state, harmonics, zone_slot, bin_list, shell_radius):
    channels, width_x, width_y, width_z = fluid_state.shape
    harm_count = harmonics.shape[0]
    zone_count = width_x * width_y * width_z
    device_count = lax.axis_size("bricks")
    flat_harm = harmonics.reshape(harm_count, zone_count)
    slot_flat = zone_slot.reshape(zone_count)
    my_bins = bin_list[0]
    listed = my_bins.shape[0]
    velocity = fluid_state[1] / fluid_state[0]
    extended = jnp.concatenate([fluid_state, velocity[None]], axis=0)
    padded = padded_2(extended.astype(jnp.bfloat16), (("bricks", 1),), 1).astype(extended.dtype)
    fractions = fluid_state[5:] / fluid_state[0][None]
    local_low = jnp.min(fractions, axis=(1, 2, 3))
    local_high = jnp.max(fractions, axis=(1, 2, 3))
    mass = fluid_state[0].reshape(zone_count).astype(jnp.bfloat16)
    selector = jnp.arange(listed, dtype=jnp.int32)[:, None] == slot_flat[None, :]
    weights = jnp.where(selector, mass[None, :], jnp.zeros((), jnp.bfloat16))
    partial_value = lax.dot_general(
        flat_harm, weights, (((1,), (1,)), ((), ())), preferred_element_type=jnp.float32
    )
    block = round_up(-(-harm_count // device_count), 8)
    padded_count = block * device_count
    parts = jnp.pad(partial_value, ((0, padded_count - harm_count), (0, 0))).reshape(
        device_count, block, listed
    )
    species = local_low.shape[0]
    extreme_row = jnp.pad(jnp.concatenate([-local_low, local_high]), (0, listed - 2 * species))
    small = jnp.pad(
        jnp.stack([my_bins.astype(jnp.float32), extreme_row]), ((0, 6), (0, 0))
    )
    own_degree = lax.dynamic_slice_in_dim(
        jnp.pad(degrees(harm_count), (0, padded_count + 128 - harm_count)),
        lax.axis_index("bricks") * block, 128)
    step_in, step_out, last_row = log_steps(shell_radius)
    first = jnp.arange(NB, dtype=jnp.int32) == 0
    grow_in = jnp.where(first[:, None], 0.0, jnp.exp((own_degree[None, :] + 1.0) * step_in[:, None]))
    grow_out = jnp.where(last_row[:, None], 0.0, jnp.exp(own_degree[None, :] * step_out[:, None]))
    radius = jnp.broadcast_to(shell_radius[:, None], (NB, 128))
    shells, extremes = exchange(parts, small, grow_in, grow_out, radius)
    lower_bound = -extremes[1, :species]
    upper_bound = extremes[1, species : 2 * species]
    shell_mine = shells[:, :block].reshape(padded_count, listed)[:harm_count].T
    product = jnp.dot(shell_mine, flat_harm, preferred_element_type=jnp.float32)
    factor = -1.0 / math.sqrt(float(HARM * zone_count * device_count))
    potential = (jnp.sum(jnp.where(selector, product, 0.0), axis=0) * factor).reshape(
        width_x, width_y, width_z
    )
    potential_padded = padded_2(potential, (("bricks", 0),), 1)
    new_state = advance(fluid_state, padded, potential_padded, lower_bound, upper_bound)
    return (new_state, potential)


def solution(mesh):
    placed = (
        P(None, "bricks", None, None),
        P(None, "bricks", None, None),
        P("bricks", None, None),
        P("bricks", None),
        P(),
    )
    return jax.shard_map(
        per_device,
        mesh=mesh,
        in_specs=placed,
        out_specs=(P(None, "bricks", None, None), P("bricks", None, None)),
        check_vma=False,
    )
```

```python
import functools
import math

import jax
import jax.numpy as jnp
from jax import lax
from jax.experimental import pallas as pl
from jax.experimental.pallas import tpu as pltpu
from jax.sharding import PartitionSpec as P

LMAX = 40
HARM = 1681
NB = 1024


MESH = pl.DeviceIdType.MESH

time_step = 0.05


def padded_2(cells, sides, width):
    for axis, dim in sides:
        count = lax.axis_size(axis)
        ends = count - 1
        head = lax.slice_in_dim(cells, 0, width, axis=dim)
        tail = lax.slice_in_dim(cells, cells.shape[dim] - width, cells.shape[dim], axis=dim)
        cells = jnp.concatenate(
            [
                lax.ppermute(tail, axis, [(i, (i + 1) % count) for i in range(ends)]),
                cells,
                lax.ppermute(head, axis, [((i + 1) % count, i) for i in range(ends)]),
            ],
            axis=dim,
        )
    return cells


def degrees(harm_count):
    numbers = jnp.arange(harm_count, dtype=jnp.int32)
    marks = jnp.arange(1, LMAX + 1, dtype=jnp.int32) ** 2
    return jnp.sum((numbers[:, None] >= marks[None, :]).astype(jnp.int32), axis=1).astype(
        jnp.float32
    )


def log_steps(radius):
    bin_count = radius.shape[0]
    step_in = jnp.concatenate(
        [jnp.zeros((1,), radius.dtype), jnp.log(radius[:-1]) - jnp.log(radius[1:])]
    )
    step_out = jnp.concatenate([step_in[1:], jnp.zeros((1,), radius.dtype)])
    last_row = jnp.arange(bin_count, dtype=jnp.int32) == bin_count - 1
    return (step_in, step_out, last_row)


def round_up(value, step):
    return -(-value // step) * step


def one_hot(bin_row, row_total, listed):
    rows = lax.broadcasted_iota(jnp.int32, (row_total, listed), 0)
    return jnp.where(rows == bin_row, 1.0, 0.0).astype(jnp.bfloat16)


INNER = 8


def exchange_kernel(
    outer, part_ref, small_ref, grow_in_ref, grow_out_ref, radius_ref,
    shell_ref, extreme_ref,
    got, smalls, marks, sum_out, sum_in, dense, sent_back, came_back, worst,
    small_send, small_recv, part_send, part_recv, sum_send, sum_recv,
    worst_send, worst_recv, dense_send, dense_recv, back_send, back_recv,
):
    me = lax.axis_index("bricks")
    place, layer = lax.rem(me, INNER), me // INNER
    block, listed = part_ref.shape[2:]
    rows = radius_ref.shape[1]
    back_rows = dense.shape[1]

    def beside(offset):
        return lax.rem(place + offset, INNER)

    def above(offset):
        return lax.rem(layer + offset, outer)

    def in_layer(spot):
        return (layer * INNER + spot,)

    def in_column(level):
        return (level * INNER + place,)

    barrier = pltpu.get_barrier_semaphore()

    def greet_layer(offset, carry):
        pl.semaphore_signal(
            barrier, inc=1, device_id=in_layer(beside(offset)), device_id_type=MESH)
        return carry

    def greet_column(offset, carry):
        pl.semaphore_signal(
            barrier, inc=1, device_id=in_column(above(offset)), device_id_type=MESH)
        return carry

    lax.fori_loop(1, INNER, greet_layer, 0)
    lax.fori_loop(1, outer, greet_column, 0)
    smalls[place] = small_ref[...]
    got[place] = part_ref[place]
    pl.semaphore_wait(barrier, INNER + outer - 2)

    def small_copy(spot, slot):
        return pltpu.make_async_remote_copy(
            src_ref=small_ref, dst_ref=smalls.at[slot], send_sem=small_send.at[spot],
            recv_sem=small_recv.at[slot], device_id=in_layer(spot), device_id_type=MESH)

    def part_copy(spot, slot, level):
        return pltpu.make_async_remote_copy(
            src_ref=part_ref.at[spot, level], dst_ref=got.at[slot, level],
            send_sem=part_send.at[spot, level], recv_sem=part_recv.at[slot, level],
            device_id=in_layer(spot), device_id_type=MESH)

    def sum_copy(level, slot):
        return pltpu.make_async_remote_copy(
            src_ref=sum_out.at[level], dst_ref=sum_in.at[slot], send_sem=sum_send.at[level],
            recv_sem=sum_recv.at[slot], device_id=in_column(level), device_id_type=MESH)

    def worst_copy(level, slot):
        return pltpu.make_async_remote_copy(
            src_ref=worst.at[layer], dst_ref=worst.at[slot], send_sem=worst_send.at[level],
            recv_sem=worst_recv.at[slot], device_id=in_column(level), device_id_type=MESH)

    def dense_copy(level, slot):
        return pltpu.make_async_remote_copy(
            src_ref=dense.at[layer], dst_ref=dense.at[slot], send_sem=dense_send.at[level],
            recv_sem=dense_recv.at[slot], device_id=in_column(level), device_id_type=MESH)

    def back_copy(spot, slot, level):
        return pltpu.make_async_remote_copy(
            src_ref=sent_back.at[spot, level], dst_ref=came_back.at[slot, level],
            send_sem=back_send.at[spot, level], recv_sem=back_recv.at[slot, level],
            device_id=in_layer(spot), device_id_type=MESH)

    def send_small(offset, carry):
        small_copy(beside(offset), place).start()
        return carry

    lax.fori_loop(1, INNER, send_small, 0)

    def send_chunk(turn, carry):
        def send(offset, carry):
            part_copy(beside(offset), place, above(turn)).start()
            return carry

        return lax.fori_loop(1, INNER, send, carry)

    lax.fori_loop(1, outer + 1, send_chunk, 0)

    def columns(spot):
        return pl.ds(pl.multiple_of(spot * listed, listed), listed)

    def mark(spot):
        marks[:, columns(spot)] = one_hot(smalls[spot, 0:1, :].astype(jnp.int32), rows, listed)

    mark(place)

    def mark_other(offset, carry):
        spot = beside(INNER - offset)
        small_copy(beside(offset), spot).wait_recv()
        mark(spot)
        return carry

    lax.fori_loop(1, INNER, mark_other, 0)
    worst[layer] = jnp.max(smalls[...], axis=0)

    def send_worst(offset, carry):
        worst_copy(above(offset), layer).start()
        return carry

    lax.fori_loop(1, outer, send_worst, 0)

    def add_chunk(turn, carry):
        level = above(turn)

        def arrive(offset, carry):
            part_copy(beside(offset), beside(INNER - offset), level).wait_recv()
            return carry

        lax.fori_loop(1, INNER, arrive, 0)
        halves = []
        for spot in range(INNER):
            values = got[spot, level]
            high = values.astype(jnp.bfloat16).astype(jnp.float32)
            gap = jnp.zeros((64 - block, listed), jnp.float32)
            halves.append(
                jnp.concatenate([high, gap, values - high, gap], axis=0).astype(jnp.bfloat16)
            )
        both = lax.dot_general(
            marks[...], jnp.concatenate(halves, axis=1),
            (((1,), (1,)), ((), ())), preferred_element_type=jnp.float32)
        sum_out[level] = (both + pltpu.roll(both, 64, 1)).T[0:block]

        @pl.when(turn < outer)
        def _():
            sum_copy(level, layer).start()

        return carry

    lax.fori_loop(1, outer + 1, add_chunk, 0)
    sum_in[layer] = sum_out[layer]

    def sum_arrives(offset, carry):
        sum_copy(above(offset), above(outer - offset)).wait_recv()
        return carry

    lax.fori_loop(1, outer, sum_arrives, 0)
    scaled = jnp.sum(sum_in[...], axis=0) / radius_ref[...]
    field = -scaled
    for grow_ref, backward in ((grow_in_ref, False), (grow_out_ref, True)):
        factor, value = grow_ref[...], scaled
        step = 1
        while step < rows:
            turn = rows - step if backward else step
            value = value + factor * pltpu.roll(value, turn, 1)
            factor = factor * pltpu.roll(factor, turn, 1)
            step *= 2
        field = field + value
    if back_rows > block:
        field = jnp.concatenate(
            [field, jnp.zeros((back_rows - block, rows), jnp.float32)], axis=0)
    dense[layer] = field.astype(jnp.bfloat16)

    def send_dense(offset, carry):
        dense_copy(above(offset), layer).start()
        return carry

    lax.fori_loop(1, outer, send_dense, 0)

    def select(spot, level):
        return jnp.dot(
            dense[level], marks[:, columns(spot)], preferred_element_type=jnp.float32
        ).astype(jnp.bfloat16)

    def give_back(turn, carry):
        level = above(outer - turn)

        @pl.when(turn > 0)
        def _():
            dense_copy(above(turn), level).wait_recv()

        def give(offset, carry):
            spot = beside(offset)
            sent_back[spot, level] = select(spot, level)
            back_copy(spot, place, level).start()
            return carry

        lax.fori_loop(1, INNER, give, 0)
        came_back[place, level] = select(place, level)
        return carry

    lax.fori_loop(0, outer, give_back, 0)

    def finish_column(offset, carry):
        level, origin = above(offset), above(outer - offset)
        sum_copy(level, layer).wait_send()
        worst_copy(level, layer).wait_send()
        dense_copy(level, layer).wait_send()
        worst_copy(level, origin).wait_recv()
        return carry

    lax.fori_loop(1, outer, finish_column, 0)
    extreme_ref[...] = jnp.max(worst[...], axis=0)

    def finish_layer(offset, carry):
        spot, origin = beside(offset), beside(INNER - offset)
        small_copy(spot, place).wait_send()

        def finish(level, carry):
            part_copy(spot, place, level).wait_send()
            back_copy(spot, place, level).wait_send()
            back_copy(spot, origin, level).wait_recv()
            return carry

        return lax.fori_loop(0, outer, finish, carry)

    lax.fori_loop(1, INNER, finish_layer, 0)
    shell_ref[...] = came_back[...]


def exchange(parts, small, grow_in, grow_out, radius):
    inner, outer, block, listed = parts.shape
    rows = radius.shape[1]
    back_rows = round_up(block, 16)
    whole = pl.BlockSpec(memory_space=pltpu.VMEM)
    dma = pltpu.SemaphoreType.DMA
    return pl.pallas_call(
        functools.partial(exchange_kernel, outer),
        out_shape=(
            jax.ShapeDtypeStruct((inner, outer, back_rows, listed), jnp.bfloat16),
            jax.ShapeDtypeStruct(small.shape, jnp.float32),
        ),
        in_specs=[whole] * 5,
        out_specs=(whole, whole),
        scratch_shapes=[
            pltpu.VMEM(parts.shape, jnp.float32),
            pltpu.VMEM((inner,) + small.shape, jnp.float32),
            pltpu.VMEM((rows, inner * listed), jnp.bfloat16),
            pltpu.VMEM((outer, block, rows), jnp.float32),
            pltpu.VMEM((outer, block, rows), jnp.float32),
            pltpu.VMEM((outer, back_rows, rows), jnp.bfloat16),
            pltpu.VMEM((inner, outer, back_rows, listed), jnp.bfloat16),
            pltpu.VMEM((inner, outer, back_rows, listed), jnp.bfloat16),
            pltpu.VMEM((outer,) + small.shape, jnp.float32),
            dma((inner,)), dma((inner,)), dma((inner, outer)), dma((inner, outer)),
            dma((outer,)), dma((outer,)), dma((outer,)), dma((outer,)),
            dma((outer,)), dma((outer,)), dma((inner, outer)), dma((inner, outer)),
        ],
        compiler_params=pltpu.CompilerParams(
            collective_id=0, has_side_effects=True, vmem_limit_bytes=48 * 1024 * 1024
        ),
    )(parts, small, grow_in, grow_out, radius)


def advance(fluid_state, padded, potential_padded, lower_bound, upper_bound):
    channels = fluid_state.shape[0]
    speed = padded[channels]
    fields = padded[:channels]
    face_flux = 0.25 * (speed[1:] + speed[:-1])[None] * (fields[:, 1:] + fields[:, :-1])
    advanced = fluid_state - time_step * (face_flux[:, 1:] - face_flux[:, :-1])
    gradient = 0.5 * (potential_padded[2:] - potential_padded[:-2])
    density = advanced[0]
    momentum = advanced[1] - time_step * fluid_state[0] * gradient
    energy = advanced[4] - time_step * fluid_state[1] * gradient
    fraction = jnp.clip(
        advanced[5:] / density[None],
        lower_bound[:, None, None, None],
        upper_bound[:, None, None, None],
    )
    return jnp.concatenate(
        [density[None], momentum[None], advanced[2:4], energy[None], density[None] * fraction],
        axis=0,
    )


def per_device(fluid_state, harmonics, zone_slot, bin_list, shell_radius):
    channels, width_x, width_y, width_z = fluid_state.shape
    harm_count = harmonics.shape[0]
    zone_count = width_x * width_y * width_z
    device_count = lax.axis_size("bricks")
    flat_harm = harmonics.reshape(harm_count, zone_count)
    slot_flat = zone_slot.reshape(zone_count)
    my_bins = bin_list[0]
    listed = my_bins.shape[0]
    velocity = fluid_state[1] / fluid_state[0]
    extended = jnp.concatenate([fluid_state, velocity[None]], axis=0)
    padded = padded_2(extended.astype(jnp.bfloat16), (("bricks", 1),), 1).astype(extended.dtype)
    fractions = fluid_state[5:] / fluid_state[0][None]
    local_low = jnp.min(fractions, axis=(1, 2, 3))
    local_high = jnp.max(fractions, axis=(1, 2, 3))
    mass = fluid_state[0].reshape(zone_count).astype(jnp.bfloat16)
    selector = jnp.arange(listed, dtype=jnp.int32)[:, None] == slot_flat[None, :]
    weights = jnp.where(selector, mass[None, :], jnp.zeros((), jnp.bfloat16))
    partial_value = lax.dot_general(
        flat_harm, weights, (((1,), (1,)), ((), ())), preferred_element_type=jnp.float32
    )
    block = round_up(-(-harm_count // device_count), 8)
    outer = device_count // INNER
    me = lax.axis_index("bricks")
    own_block = lax.rem(me, INNER) * outer + me // INNER
    padded_count = block * device_count
    parts = jnp.pad(partial_value, ((0, padded_count - harm_count), (0, 0))).reshape(
        INNER, outer, block, listed
    )
    species = local_low.shape[0]
    extreme_row = jnp.pad(jnp.concatenate([-local_low, local_high]), (0, listed - 2 * species))
    small = jnp.pad(
        jnp.stack([my_bins.astype(jnp.float32), extreme_row]), ((0, 6), (0, 0))
    )
    own_degree = lax.dynamic_slice_in_dim(
        jnp.pad(degrees(harm_count), (0, padded_count - harm_count)), own_block * block, block)
    step_in, step_out, last_row = log_steps(shell_radius)
    first = jnp.arange(NB, dtype=jnp.int32) == 0
    grow_in = jnp.where(first[None, :], 0.0, jnp.exp((own_degree[:, None] + 1.0) * step_in[None, :]))
    grow_out = jnp.where(last_row[None, :], 0.0, jnp.exp(own_degree[:, None] * step_out[None, :]))
    radius = shell_radius[None, :]
    shells, extremes = exchange(parts, small, grow_in, grow_out, radius)
    lower_bound = -extremes[1, :species]
    upper_bound = extremes[1, species : 2 * species]
    shell_mine = shells[:, :, :block].reshape(padded_count, listed)[:harm_count].T
    product = jnp.dot(shell_mine, flat_harm, preferred_element_type=jnp.float32)
    factor = -1.0 / math.sqrt(float(HARM * zone_count * device_count))
    potential = (jnp.sum(jnp.where(selector, product, 0.0), axis=0) * factor).reshape(
        width_x, width_y, width_z
    )
    potential_padded = padded_2(potential, (("bricks", 0),), 1)
    new_state = advance(fluid_state, padded, potential_padded, lower_bound, upper_bound)
    return (new_state, potential)


def solution(mesh):
    placed = (
        P(None, "bricks", None, None),
        P(None, "bricks", None, None),
        P("bricks", None, None),
        P("bricks", None),
        P(),
    )
    return jax.shard_map(
        per_device,
        mesh=mesh,
        in_specs=placed,
        out_specs=(P(None, "bricks", None, None), P("bricks", None, None)),
        check_vma=False,
    )
```

```python
import functools
import math

import jax
import jax.numpy as jnp
from jax import lax
from jax.experimental import pallas as pl
from jax.experimental.pallas import tpu as pltpu
from jax.sharding import PartitionSpec as P

LMAX = 40
HARM = 1681
NB = 1024


MESH = pl.DeviceIdType.MESH

time_step = 0.05


def padded_2(cells, sides, width):
    for axis, dim in sides:
        count = lax.axis_size(axis)
        ends = count - 1
        head = lax.slice_in_dim(cells, 0, width, axis=dim)
        tail = lax.slice_in_dim(cells, cells.shape[dim] - width, cells.shape[dim], axis=dim)
        cells = jnp.concatenate(
            [
                lax.ppermute(tail, axis, [(i, (i + 1) % count) for i in range(ends)]),
                cells,
                lax.ppermute(head, axis, [((i + 1) % count, i) for i in range(ends)]),
            ],
            axis=dim,
        )
    return cells


def degrees(harm_count):
    numbers = jnp.arange(harm_count, dtype=jnp.int32)
    marks = jnp.arange(1, LMAX + 1, dtype=jnp.int32) ** 2
    return jnp.sum((numbers[:, None] >= marks[None, :]).astype(jnp.int32), axis=1).astype(
        jnp.float32
    )


def log_steps(radius):
    bin_count = radius.shape[0]
    step_in = jnp.concatenate(
        [jnp.zeros((1,), radius.dtype), jnp.log(radius[:-1]) - jnp.log(radius[1:])]
    )
    step_out = jnp.concatenate([step_in[1:], jnp.zeros((1,), radius.dtype)])
    last_row = jnp.arange(bin_count, dtype=jnp.int32) == bin_count - 1
    return (step_in, step_out, last_row)


def round_up(value, step):
    return -(-value // step) * step


def one_hot(bin_row, row_total, listed):
    rows = lax.broadcasted_iota(jnp.int32, (row_total, listed), 0)
    return jnp.where(rows == bin_row, 1.0, 0.0).astype(jnp.bfloat16)


INNER = 8


def exchange_kernel(
    outer, part_ref, small_ref, grow_in_ref, grow_out_ref, radius_ref, edge_ref,
    shell_ref, extreme_ref, halo_ref,
    got, smalls, marks, sum_out, sum_in, dense, sent_back, came_back, worst, halo,
    small_send, small_recv, part_send, part_recv, sum_send, sum_recv,
    worst_send, worst_recv, dense_send, dense_recv, back_send, back_recv,
    edge_send, edge_recv,
):
    me = lax.axis_index("bricks")
    place, layer = lax.rem(me, INNER), me // INNER
    block, listed = part_ref.shape[2:]
    rows = radius_ref.shape[1]
    back_rows = dense.shape[1]

    def beside(offset):
        return lax.rem(place + offset, INNER)

    def above(offset):
        return lax.rem(layer + offset, outer)

    def in_layer(spot):
        return (layer * INNER + spot,)

    def in_column(level):
        return (level * INNER + place,)

    barrier = pltpu.get_barrier_semaphore()

    def greet_layer(offset, carry):
        pl.semaphore_signal(
            barrier, inc=1, device_id=in_layer(beside(offset)), device_id_type=MESH)
        return carry

    def greet_column(offset, carry):
        pl.semaphore_signal(
            barrier, inc=1, device_id=in_column(above(offset)), device_id_type=MESH)
        return carry

    count = outer * INNER
    ring = ((lax.rem(me + count - 1, count),), (lax.rem(me + 1, count),))
    for neighbour in ring:
        pl.semaphore_signal(barrier, inc=1, device_id=neighbour, device_id_type=MESH)
    lax.fori_loop(1, INNER, greet_layer, 0)
    lax.fori_loop(1, outer, greet_column, 0)
    smalls[place] = small_ref[...]
    got[place] = part_ref[place]
    pl.semaphore_wait(barrier, INNER + outer)

    def small_copy(spot, slot):
        return pltpu.make_async_remote_copy(
            src_ref=small_ref, dst_ref=smalls.at[slot], send_sem=small_send.at[spot],
            recv_sem=small_recv.at[slot], device_id=in_layer(spot), device_id_type=MESH)

    def part_copy(spot, slot, level):
        return pltpu.make_async_remote_copy(
            src_ref=part_ref.at[spot, level], dst_ref=got.at[slot, level],
            send_sem=part_send.at[spot, level], recv_sem=part_recv.at[slot, level],
            device_id=in_layer(spot), device_id_type=MESH)

    def sum_copy(level, slot):
        return pltpu.make_async_remote_copy(
            src_ref=sum_out.at[level], dst_ref=sum_in.at[slot], send_sem=sum_send.at[level],
            recv_sem=sum_recv.at[slot], device_id=in_column(level), device_id_type=MESH)

    def worst_copy(level, slot):
        return pltpu.make_async_remote_copy(
            src_ref=worst.at[layer], dst_ref=worst.at[slot], send_sem=worst_send.at[level],
            recv_sem=worst_recv.at[slot], device_id=in_column(level), device_id_type=MESH)

    def dense_copy(level, slot):
        return pltpu.make_async_remote_copy(
            src_ref=dense.at[layer], dst_ref=dense.at[slot], send_sem=dense_send.at[level],
            recv_sem=dense_recv.at[slot], device_id=in_column(level), device_id_type=MESH)

    def back_copy(spot, slot, level):
        return pltpu.make_async_remote_copy(
            src_ref=sent_back.at[spot, level], dst_ref=came_back.at[slot, level],
            send_sem=back_send.at[spot, level], recv_sem=back_recv.at[slot, level],
            device_id=in_layer(spot), device_id_type=MESH)

    edges = [
        pltpu.make_async_remote_copy(
            src_ref=edge_ref.at[side], dst_ref=halo.at[1 - side], send_sem=edge_send.at[side],
            recv_sem=edge_recv.at[1 - side], device_id=ring[side], device_id_type=MESH)
        for side in range(2)
    ]

    def send_small(offset, carry):
        small_copy(beside(offset), place).start()
        return carry

    lax.fori_loop(1, INNER, send_small, 0)

    def send_chunk(turn, carry):
        def send(offset, carry):
            part_copy(beside(offset), place, above(turn)).start()
            return carry

        return lax.fori_loop(1, INNER, send, carry)

    lax.fori_loop(1, outer + 1, send_chunk, 0)

    for edge in edges:
        edge.start()

    def columns(spot):
        return pl.ds(pl.multiple_of(spot * listed, listed), listed)

    def mark(spot):
        marks[:, columns(spot)] = one_hot(smalls[spot, 0:1, :].astype(jnp.int32), rows, listed)

    mark(place)

    def mark_other(offset, carry):
        spot = beside(INNER - offset)
        small_copy(beside(offset), spot).wait_recv()
        mark(spot)
        return carry

    lax.fori_loop(1, INNER, mark_other, 0)
    worst[layer] = jnp.max(smalls[...], axis=0)

    def send_worst(offset, carry):
        worst_copy(above(offset), layer).start()
        return carry

    lax.fori_loop(1, outer, send_worst, 0)

    def add_chunk(turn, carry):
        level = above(turn)

        def arrive(offset, carry):
            part_copy(beside(offset), beside(INNER - offset), level).wait_recv()
            return carry

        lax.fori_loop(1, INNER, arrive, 0)
        halves = []
        for spot in range(INNER):
            values = got[spot, level]
            high = values.astype(jnp.bfloat16).astype(jnp.float32)
            gap = jnp.zeros((64 - block, listed), jnp.float32)
            halves.append(
                jnp.concatenate([high, gap, values - high, gap], axis=0).astype(jnp.bfloat16)
            )
        both = lax.dot_general(
            marks[...], jnp.concatenate(halves, axis=1),
            (((1,), (1,)), ((), ())), preferred_element_type=jnp.float32)
        sum_out[level] = (both + pltpu.roll(both, 64, 1)).T[0:block]

        @pl.when(turn < outer)
        def _():
            sum_copy(level, layer).start()

        return carry

    lax.fori_loop(1, outer + 1, add_chunk, 0)
    sum_in[layer] = sum_out[layer]

    def sum_arrives(offset, carry):
        sum_copy(above(offset), above(outer - offset)).wait_recv()
        return carry

    lax.fori_loop(1, outer, sum_arrives, 0)
    scaled = jnp.sum(sum_in[...], axis=0) / radius_ref[...]
    field = -scaled
    for grow_ref, backward in ((grow_in_ref, False), (grow_out_ref, True)):
        factor, value = grow_ref[...], scaled
        step = 1
        while step < rows:
            turn = rows - step if backward else step
            value = value + factor * pltpu.roll(value, turn, 1)
            factor = factor * pltpu.roll(factor, turn, 1)
            step *= 2
        field = field + value
    if back_rows > block:
        field = jnp.concatenate(
            [field, jnp.zeros((back_rows - block, rows), jnp.float32)], axis=0)
    dense[layer] = field.astype(jnp.bfloat16)

    def send_dense(offset, carry):
        dense_copy(above(offset), layer).start()
        return carry

    lax.fori_loop(1, outer, send_dense, 0)

    def select(spot, level):
        return jnp.dot(
            dense[level], marks[:, columns(spot)], preferred_element_type=jnp.float32
        ).astype(jnp.bfloat16)

    def give_back(turn, carry):
        level = above(outer - turn)

        @pl.when(turn > 0)
        def _():
            dense_copy(above(turn), level).wait_recv()

        def give(offset, carry):
            spot = beside(offset)
            sent_back[spot, level] = select(spot, level)
            back_copy(spot, place, level).start()
            return carry

        lax.fori_loop(1, INNER, give, 0)
        came_back[place, level] = select(place, level)
        return carry

    lax.fori_loop(0, outer, give_back, 0)

    def finish_column(offset, carry):
        level, origin = above(offset), above(outer - offset)
        sum_copy(level, layer).wait_send()
        worst_copy(level, layer).wait_send()
        dense_copy(level, layer).wait_send()
        worst_copy(level, origin).wait_recv()
        return carry

    lax.fori_loop(1, outer, finish_column, 0)
    extreme_ref[...] = jnp.max(worst[...], axis=0)

    def finish_layer(offset, carry):
        spot, origin = beside(offset), beside(INNER - offset)
        small_copy(spot, place).wait_send()

        def finish(level, carry):
            part_copy(spot, place, level).wait_send()
            back_copy(spot, place, level).wait_send()
            back_copy(spot, origin, level).wait_recv()
            return carry

        return lax.fori_loop(0, outer, finish, carry)

    lax.fori_loop(1, INNER, finish_layer, 0)
    shell_ref[...] = came_back[...]
    for edge in edges:
        edge.wait()
    halo_ref[...] = halo[...]


def exchange(parts, small, grow_in, grow_out, radius, edges):
    inner, outer, block, listed = parts.shape
    rows = radius.shape[1]
    back_rows = round_up(block, 16)
    whole = pl.BlockSpec(memory_space=pltpu.VMEM)
    dma = pltpu.SemaphoreType.DMA
    return pl.pallas_call(
        functools.partial(exchange_kernel, outer),
        out_shape=(
            jax.ShapeDtypeStruct((inner, outer, back_rows, listed), jnp.bfloat16),
            jax.ShapeDtypeStruct(small.shape, jnp.float32),
            jax.ShapeDtypeStruct(edges.shape, edges.dtype),
        ),
        in_specs=[whole] * 6,
        out_specs=(whole, whole, whole),
        scratch_shapes=[
            pltpu.VMEM(parts.shape, jnp.float32),
            pltpu.VMEM((inner,) + small.shape, jnp.float32),
            pltpu.VMEM((rows, inner * listed), jnp.bfloat16),
            pltpu.VMEM((outer, block, rows), jnp.float32),
            pltpu.VMEM((outer, block, rows), jnp.float32),
            pltpu.VMEM((outer, back_rows, rows), jnp.bfloat16),
            pltpu.VMEM((inner, outer, back_rows, listed), jnp.bfloat16),
            pltpu.VMEM((inner, outer, back_rows, listed), jnp.bfloat16),
            pltpu.VMEM((outer,) + small.shape, jnp.float32),
            pltpu.VMEM(edges.shape, edges.dtype),
            dma((inner,)), dma((inner,)), dma((inner, outer)), dma((inner, outer)),
            dma((outer,)), dma((outer,)), dma((outer,)), dma((outer,)),
            dma((outer,)), dma((outer,)), dma((inner, outer)), dma((inner, outer)),
            dma((2,)), dma((2,)),
        ],
        compiler_params=pltpu.CompilerParams(
            collective_id=0, has_side_effects=True, vmem_limit_bytes=48 * 1024 * 1024
        ),
    )(parts, small, grow_in, grow_out, radius, edges)


TILE = 224


def moment_kernel(harm_count, harm_ref, weight_ref, flat_ref, part_ref):
    tile, lines, width = harm_ref.shape
    values = harm_ref[...].reshape(tile, lines * width)
    flat_ref[...] = values
    sums = jnp.dot(values, weight_ref[...], preferred_element_type=jnp.float32)
    number = pl.program_id(0) * tile + lax.broadcasted_iota(jnp.int32, sums.shape, 0)
    part_ref[...] = jnp.where(number < harm_count, sums, 0.0)


def flat_and_moments(harm, weights):
    harm_count, lines, width = harm.shape
    zone_count, listed = weights.shape
    steps = -(-harm_count // TILE)
    return pl.pallas_call(
        functools.partial(moment_kernel, harm_count),
        grid=(steps,),
        out_shape=(
            jax.ShapeDtypeStruct((harm_count, zone_count), harm.dtype),
            jax.ShapeDtypeStruct((steps * TILE, listed), jnp.float32),
        ),
        in_specs=[
            pl.BlockSpec((TILE, lines, width), lambda i: (i, 0, 0)),
            pl.BlockSpec((zone_count, listed), lambda i: (0, 0)),
        ],
        out_specs=(
            pl.BlockSpec((TILE, zone_count), lambda i: (i, 0)),
            pl.BlockSpec((TILE, listed), lambda i: (i, 0)),
        ),
        compiler_params=pltpu.CompilerParams(vmem_limit_bytes=48 * 1024 * 1024),
    )(harm, weights)


def advance(fluid_state, padded, potential_padded, lower_bound, upper_bound):
    channels = fluid_state.shape[0]
    speed = padded[channels]
    fields = padded[:channels]
    face_flux = 0.25 * (speed[1:] + speed[:-1])[None] * (fields[:, 1:] + fields[:, :-1])
    advanced = fluid_state - time_step * (face_flux[:, 1:] - face_flux[:, :-1])
    gradient = 0.5 * (potential_padded[2:] - potential_padded[:-2])
    density = advanced[0]
    momentum = advanced[1] - time_step * fluid_state[0] * gradient
    energy = advanced[4] - time_step * fluid_state[1] * gradient
    fraction = jnp.clip(
        advanced[5:] / density[None],
        lower_bound[:, None, None, None],
        upper_bound[:, None, None, None],
    )
    return jnp.concatenate(
        [density[None], momentum[None], advanced[2:4], energy[None], density[None] * fraction],
        axis=0,
    )


def per_device(fluid_state, harmonics, zone_slot, bin_list, shell_radius):
    channels, width_x, width_y, width_z = fluid_state.shape
    harm_count = harmonics.shape[0]
    zone_count = width_x * width_y * width_z
    device_count = lax.axis_size("bricks")
    slot_flat = zone_slot.reshape(zone_count)
    my_bins = bin_list[0]
    listed = my_bins.shape[0]
    velocity = fluid_state[1] / fluid_state[0]
    extended = jnp.concatenate([fluid_state, velocity[None]], axis=0)
    rounded = extended.astype(jnp.bfloat16)
    edges = jnp.stack([rounded[:, 0], rounded[:, -1]]).reshape(2, -1, width_z)
    line_count = edges.shape[1]
    edges = jnp.pad(edges, ((0, 0), (0, -line_count % 16), (0, 0)))
    fractions = fluid_state[5:] / fluid_state[0][None]
    local_low = jnp.min(fractions, axis=(1, 2, 3))
    local_high = jnp.max(fractions, axis=(1, 2, 3))
    mass = fluid_state[0].reshape(zone_count).astype(jnp.bfloat16)
    selector = jnp.arange(listed, dtype=jnp.int32)[:, None] == slot_flat[None, :]
    weights = jnp.where(
        slot_flat[:, None] == jnp.arange(listed, dtype=jnp.int32)[None, :],
        mass[:, None], jnp.zeros((), jnp.bfloat16))
    flat_harm, partial_value = flat_and_moments(
        harmonics.reshape(harm_count, width_x * width_y, width_z), weights)
    block = round_up(-(-harm_count // device_count), 8)
    outer = device_count // INNER
    me = lax.axis_index("bricks")
    own_block = lax.rem(me, INNER) * outer + me // INNER
    padded_count = block * device_count
    spare = max(padded_count - partial_value.shape[0], 0)
    parts = jnp.pad(partial_value, ((0, spare), (0, 0)))[:padded_count].reshape(
        INNER, outer, block, listed
    )
    species = local_low.shape[0]
    extreme_row = jnp.pad(jnp.concatenate([-local_low, local_high]), (0, listed - 2 * species))
    small = jnp.pad(
        jnp.stack([my_bins.astype(jnp.float32), extreme_row]), ((0, 6), (0, 0))
    )
    own_degree = lax.dynamic_slice_in_dim(
        jnp.pad(degrees(harm_count), (0, padded_count - harm_count)), own_block * block, block)
    step_in, step_out, last_row = log_steps(shell_radius)
    first = jnp.arange(NB, dtype=jnp.int32) == 0
    grow_in = jnp.where(first[None, :], 0.0, jnp.exp((own_degree[:, None] + 1.0) * step_in[None, :]))
    grow_out = jnp.where(last_row[None, :], 0.0, jnp.exp(own_degree[:, None] * step_out[None, :]))
    radius = shell_radius[None, :]
    shells, extremes, halo = exchange(parts, small, grow_in, grow_out, radius, edges)
    halo = halo[:, :line_count].reshape(2, channels + 1, 1, width_y, width_z)
    below = jnp.where(me > 0, halo[0], jnp.zeros_like(halo[0]))
    beyond = jnp.where(me < device_count - 1, halo[1], jnp.zeros_like(halo[1]))
    padded = jnp.concatenate([below, rounded, beyond], axis=1).astype(extended.dtype)
    lower_bound = -extremes[1, :species]
    upper_bound = extremes[1, species : 2 * species]
    shell_mine = shells[:, :, :block].reshape(padded_count, listed)[:harm_count].T
    product = jnp.dot(shell_mine, flat_harm, preferred_element_type=jnp.float32)
    factor = -1.0 / math.sqrt(float(HARM * zone_count * device_count))
    potential = (jnp.sum(jnp.where(selector, product, 0.0), axis=0) * factor).reshape(
        width_x, width_y, width_z
    )
    potential_padded = padded_2(potential, (("bricks", 0),), 1)
    new_state = advance(fluid_state, padded, potential_padded, lower_bound, upper_bound)
    return (new_state, potential)


def solution(mesh):
    placed = (
        P(None, "bricks", None, None),
        P(None, "bricks", None, None),
        P("bricks", None, None),
        P("bricks", None),
        P(),
    )
    return jax.shard_map(
        per_device,
        mesh=mesh,
        in_specs=placed,
        out_specs=(P(None, "bricks", None, None), P("bricks", None, None)),
        check_vma=False,
    )
```

```python
import functools
import math

import jax
import jax.numpy as jnp
from jax import lax
from jax.experimental import pallas as pl
from jax.experimental.pallas import tpu as pltpu
from jax.sharding import PartitionSpec as P

LMAX = 40
HARM = 1681
NB = 1024


MESH = pl.DeviceIdType.MESH

time_step = 0.05


def padded_2(cells, sides, width):
    for axis, dim in sides:
        count = lax.axis_size(axis)
        ends = count - 1
        head = lax.slice_in_dim(cells, 0, width, axis=dim)
        tail = lax.slice_in_dim(cells, cells.shape[dim] - width, cells.shape[dim], axis=dim)
        cells = jnp.concatenate(
            [
                lax.ppermute(tail, axis, [(i, (i + 1) % count) for i in range(ends)]),
                cells,
                lax.ppermute(head, axis, [((i + 1) % count, i) for i in range(ends)]),
            ],
            axis=dim,
        )
    return cells


def degrees(harm_count):
    numbers = jnp.arange(harm_count, dtype=jnp.int32)
    marks = jnp.arange(1, LMAX + 1, dtype=jnp.int32) ** 2
    return jnp.sum((numbers[:, None] >= marks[None, :]).astype(jnp.int32), axis=1).astype(
        jnp.float32
    )


def log_steps(radius):
    bin_count = radius.shape[0]
    step_in = jnp.concatenate(
        [jnp.zeros((1,), radius.dtype), jnp.log(radius[:-1]) - jnp.log(radius[1:])]
    )
    step_out = jnp.concatenate([step_in[1:], jnp.zeros((1,), radius.dtype)])
    last_row = jnp.arange(bin_count, dtype=jnp.int32) == bin_count - 1
    return (step_in, step_out, last_row)


def round_up(value, step):
    return -(-value // step) * step


def one_hot(bin_row, row_total, listed):
    rows = lax.broadcasted_iota(jnp.int32, (row_total, listed), 0)
    return jnp.where(rows == bin_row, 1.0, 0.0).astype(jnp.bfloat16)


INNER = 8


def exchange_kernel(
    outer, part_ref, small_ref, grow_in_ref, grow_out_ref, radius_ref, edge_ref,
    shell_ref, extreme_ref, halo_ref,
    got, smalls, marks, sum_out, sum_in, dense, sent_back, came_back, worst, halo,
    small_send, small_recv, part_send, part_recv, sum_send, sum_recv,
    worst_send, worst_recv, dense_send, dense_recv, back_send, back_recv,
    edge_send, edge_recv,
):
    me = lax.axis_index("bricks")
    place, layer = lax.rem(me, INNER), me // INNER
    block, listed = part_ref.shape[2:]
    rows = radius_ref.shape[1]
    back_rows = dense.shape[1]

    def beside(offset):
        return lax.rem(place + offset, INNER)

    def above(offset):
        return lax.rem(layer + offset, outer)

    def in_layer(spot):
        return (layer * INNER + spot,)

    def in_column(level):
        return (level * INNER + place,)

    barrier = pltpu.get_barrier_semaphore()

    def greet_layer(offset, carry):
        pl.semaphore_signal(
            barrier, inc=1, device_id=in_layer(beside(offset)), device_id_type=MESH)
        return carry

    def greet_column(offset, carry):
        pl.semaphore_signal(
            barrier, inc=1, device_id=in_column(above(offset)), device_id_type=MESH)
        return carry

    count = outer * INNER
    ring = ((lax.rem(me + count - 1, count),), (lax.rem(me + 1, count),))
    for neighbour in ring:
        pl.semaphore_signal(barrier, inc=1, device_id=neighbour, device_id_type=MESH)
    lax.fori_loop(1, INNER, greet_layer, 0)
    lax.fori_loop(1, outer, greet_column, 0)
    smalls[place] = small_ref[...]
    got[place] = part_ref[place]
    pl.semaphore_wait(barrier, INNER + outer)

    def small_copy(spot, slot):
        return pltpu.make_async_remote_copy(
            src_ref=small_ref, dst_ref=smalls.at[slot], send_sem=small_send.at[spot],
            recv_sem=small_recv.at[slot], device_id=in_layer(spot), device_id_type=MESH)

    def part_copy(spot, slot, level):
        return pltpu.make_async_remote_copy(
            src_ref=part_ref.at[spot, level], dst_ref=got.at[slot, level],
            send_sem=part_send.at[spot, level], recv_sem=part_recv.at[slot, level],
            device_id=in_layer(spot), device_id_type=MESH)

    def sum_copy(level, slot):
        return pltpu.make_async_remote_copy(
            src_ref=sum_out.at[level], dst_ref=sum_in.at[slot], send_sem=sum_send.at[level],
            recv_sem=sum_recv.at[slot], device_id=in_column(level), device_id_type=MESH)

    def worst_copy(level, slot):
        return pltpu.make_async_remote_copy(
            src_ref=worst.at[layer], dst_ref=worst.at[slot], send_sem=worst_send.at[level],
            recv_sem=worst_recv.at[slot], device_id=in_column(level), device_id_type=MESH)

    def dense_copy(level, slot):
        return pltpu.make_async_remote_copy(
            src_ref=dense.at[layer], dst_ref=dense.at[slot], send_sem=dense_send.at[level],
            recv_sem=dense_recv.at[slot], device_id=in_column(level), device_id_type=MESH)

    def back_copy(spot, slot, level):
        return pltpu.make_async_remote_copy(
            src_ref=sent_back.at[spot, level], dst_ref=came_back.at[slot, level],
            send_sem=back_send.at[spot, level], recv_sem=back_recv.at[slot, level],
            device_id=in_layer(spot), device_id_type=MESH)

    edges = [
        pltpu.make_async_remote_copy(
            src_ref=edge_ref.at[side], dst_ref=halo.at[1 - side], send_sem=edge_send.at[side],
            recv_sem=edge_recv.at[1 - side], device_id=ring[side], device_id_type=MESH)
        for side in range(2)
    ]

    def send_small(offset, carry):
        small_copy(beside(offset), place).start()
        return carry

    lax.fori_loop(1, INNER, send_small, 0)

    def send_chunk(turn, carry):
        def send(offset, carry):
            part_copy(beside(offset), place, above(turn)).start()
            return carry

        return lax.fori_loop(1, INNER, send, carry)

    lax.fori_loop(1, outer + 1, send_chunk, 0)

    for edge in edges:
        edge.start()

    def columns(spot):
        return pl.ds(pl.multiple_of(spot * listed, listed), listed)

    def mark(spot):
        marks[:, columns(spot)] = one_hot(smalls[spot, 0:1, :].astype(jnp.int32), rows, listed)

    mark(place)

    def mark_other(offset, carry):
        spot = beside(INNER - offset)
        small_copy(beside(offset), spot).wait_recv()
        mark(spot)
        return carry

    lax.fori_loop(1, INNER, mark_other, 0)
    worst[layer] = jnp.max(smalls[...], axis=0)

    def send_worst(offset, carry):
        worst_copy(above(offset), layer).start()
        return carry

    lax.fori_loop(1, outer, send_worst, 0)

    def add_chunk(turn, carry):
        level = above(turn)

        def arrive(offset, carry):
            part_copy(beside(offset), beside(INNER - offset), level).wait_recv()
            return carry

        lax.fori_loop(1, INNER, arrive, 0)
        halves = []
        for spot in range(INNER):
            values = got[spot, level]
            high = values.astype(jnp.bfloat16).astype(jnp.float32)
            gap = jnp.zeros((64 - block, listed), jnp.float32)
            halves.append(
                jnp.concatenate([high, gap, values - high, gap], axis=0).astype(jnp.bfloat16)
            )
        both = lax.dot_general(
            marks[...], jnp.concatenate(halves, axis=1),
            (((1,), (1,)), ((), ())), preferred_element_type=jnp.float32)
        sum_out[level] = (both + pltpu.roll(both, 64, 1)).T[0:block]

        @pl.when(turn < outer)
        def _():
            sum_copy(level, layer).start()

        return carry

    lax.fori_loop(1, outer + 1, add_chunk, 0)
    sum_in[layer] = sum_out[layer]

    def sum_arrives(offset, carry):
        sum_copy(above(offset), above(outer - offset)).wait_recv()
        return carry

    lax.fori_loop(1, outer, sum_arrives, 0)
    scaled = jnp.sum(sum_in[...], axis=0) / radius_ref[...]
    field = -scaled
    for grow_ref, backward in ((grow_in_ref, False), (grow_out_ref, True)):
        factor, value = grow_ref[...], scaled
        step = 1
        while step < rows:
            turn = rows - step if backward else step
            value = value + factor * pltpu.roll(value, turn, 1)
            factor = factor * pltpu.roll(factor, turn, 1)
            step *= 2
        field = field + value
    if back_rows > block:
        field = jnp.concatenate(
            [field, jnp.zeros((back_rows - block, rows), jnp.float32)], axis=0)
    dense[layer] = field.astype(jnp.bfloat16)

    def send_dense(offset, carry):
        dense_copy(above(offset), layer).start()
        return carry

    lax.fori_loop(1, outer, send_dense, 0)

    def select(spot, level):
        return jnp.dot(
            dense[level], marks[:, columns(spot)], preferred_element_type=jnp.float32
        ).astype(jnp.bfloat16)

    def give_back(turn, carry):
        level = above(outer - turn)

        @pl.when(turn > 0)
        def _():
            dense_copy(above(turn), level).wait_recv()

        def give(offset, carry):
            spot = beside(offset)
            sent_back[spot, level] = select(spot, level)
            back_copy(spot, place, level).start()
            return carry

        lax.fori_loop(1, INNER, give, 0)
        came_back[place, level] = select(place, level)
        return carry

    lax.fori_loop(0, outer, give_back, 0)

    def finish_column(offset, carry):
        level, origin = above(offset), above(outer - offset)
        sum_copy(level, layer).wait_send()
        worst_copy(level, layer).wait_send()
        dense_copy(level, layer).wait_send()
        worst_copy(level, origin).wait_recv()
        return carry

    lax.fori_loop(1, outer, finish_column, 0)
    extreme_ref[...] = jnp.max(worst[...], axis=0)

    def finish_layer(offset, carry):
        spot, origin = beside(offset), beside(INNER - offset)
        small_copy(spot, place).wait_send()

        def finish(level, carry):
            part_copy(spot, place, level).wait_send()
            back_copy(spot, place, level).wait_send()
            back_copy(spot, origin, level).wait_recv()
            return carry

        return lax.fori_loop(0, outer, finish, carry)

    lax.fori_loop(1, INNER, finish_layer, 0)
    shell_ref[...] = came_back[...]
    for edge in edges:
        edge.wait()
    halo_ref[...] = halo[...]


def exchange(parts, small, grow_in, grow_out, radius, edges):
    inner, outer, block, listed = parts.shape
    rows = radius.shape[1]
    back_rows = round_up(block, 16)
    whole = pl.BlockSpec(memory_space=pltpu.VMEM)
    dma = pltpu.SemaphoreType.DMA
    return pl.pallas_call(
        functools.partial(exchange_kernel, outer),
        out_shape=(
            jax.ShapeDtypeStruct((inner, outer, back_rows, listed), jnp.bfloat16),
            jax.ShapeDtypeStruct(small.shape, jnp.float32),
            jax.ShapeDtypeStruct(edges.shape, edges.dtype),
        ),
        in_specs=[whole] * 6,
        out_specs=(whole, whole, whole),
        scratch_shapes=[
            pltpu.VMEM(parts.shape, jnp.float32),
            pltpu.VMEM((inner,) + small.shape, jnp.float32),
            pltpu.VMEM((rows, inner * listed), jnp.bfloat16),
            pltpu.VMEM((outer, block, rows), jnp.float32),
            pltpu.VMEM((outer, block, rows), jnp.float32),
            pltpu.VMEM((outer, back_rows, rows), jnp.bfloat16),
            pltpu.VMEM((inner, outer, back_rows, listed), jnp.bfloat16),
            pltpu.VMEM((inner, outer, back_rows, listed), jnp.bfloat16),
            pltpu.VMEM((outer,) + small.shape, jnp.float32),
            pltpu.VMEM(edges.shape, edges.dtype),
            dma((inner,)), dma((inner,)), dma((inner, outer)), dma((inner, outer)),
            dma((outer,)), dma((outer,)), dma((outer,)), dma((outer,)),
            dma((outer,)), dma((outer,)), dma((inner, outer)), dma((inner, outer)),
            dma((2,)), dma((2,)),
        ],
        compiler_params=pltpu.CompilerParams(
            collective_id=0, has_side_effects=True, vmem_limit_bytes=28 * 1024 * 1024
        ),
    )(parts, small, grow_in, grow_out, radius, edges)


TILE = 224


def moment_kernel(harm_count, harm_ref, weight_ref, flat_ref, part_ref):
    tile, lines, width = harm_ref.shape
    values = harm_ref[...].reshape(tile, lines * width)
    flat_ref[...] = values
    sums = jnp.dot(values, weight_ref[...], preferred_element_type=jnp.float32)
    number = pl.program_id(0) * tile + lax.broadcasted_iota(jnp.int32, sums.shape, 0)
    part_ref[...] = jnp.where(number < harm_count, sums, 0.0)


def flat_and_moments(harm, weights):
    harm_count, lines, width = harm.shape
    zone_count, listed = weights.shape
    steps = -(-harm_count // TILE)
    return pl.pallas_call(
        functools.partial(moment_kernel, harm_count),
        grid=(steps,),
        out_shape=(
            jax.ShapeDtypeStruct((harm_count, zone_count), harm.dtype),
            jax.ShapeDtypeStruct((steps * TILE, listed), jnp.float32),
        ),
        in_specs=[
            pl.BlockSpec((TILE, lines, width), lambda i: (i, 0, 0)),
            pl.BlockSpec((zone_count, listed), lambda i: (0, 0)),
        ],
        out_specs=(
            pl.BlockSpec((TILE, zone_count), lambda i: (i, 0)),
            pl.BlockSpec((TILE, listed), lambda i: (i, 0)),
        ),
        compiler_params=pltpu.CompilerParams(vmem_limit_bytes=28 * 1024 * 1024),
    )(harm, weights)


def advance(fluid_state, padded, potential_padded, lower_bound, upper_bound):
    channels = fluid_state.shape[0]
    speed = padded[channels]
    fields = padded[:channels]
    face_flux = 0.25 * (speed[1:] + speed[:-1])[None] * (fields[:, 1:] + fields[:, :-1])
    advanced = fluid_state - time_step * (face_flux[:, 1:] - face_flux[:, :-1])
    gradient = 0.5 * (potential_padded[2:] - potential_padded[:-2])
    density = advanced[0]
    momentum = advanced[1] - time_step * fluid_state[0] * gradient
    energy = advanced[4] - time_step * fluid_state[1] * gradient
    fraction = jnp.clip(
        advanced[5:] / density[None],
        lower_bound[:, None, None, None],
        upper_bound[:, None, None, None],
    )
    return jnp.concatenate(
        [density[None], momentum[None], advanced[2:4], energy[None], density[None] * fraction],
        axis=0,
    )


def per_device(fluid_state, harmonics, zone_slot, bin_list, shell_radius):
    channels, width_x, width_y, width_z = fluid_state.shape
    harm_count = harmonics.shape[0]
    zone_count = width_x * width_y * width_z
    device_count = lax.axis_size("bricks")
    slot_flat = zone_slot.reshape(zone_count)
    my_bins = bin_list[0]
    listed = my_bins.shape[0]
    velocity = fluid_state[1] / fluid_state[0]
    extended = jnp.concatenate([fluid_state, velocity[None]], axis=0)
    rounded = extended.astype(jnp.bfloat16)
    edges = jnp.stack([rounded[:, 0], rounded[:, -1]]).reshape(2, -1, width_z)
    line_count = edges.shape[1]
    edges = jnp.pad(edges, ((0, 0), (0, -line_count % 16), (0, 0)))
    fractions = fluid_state[5:] / fluid_state[0][None]
    local_low = jnp.min(fractions, axis=(1, 2, 3))
    local_high = jnp.max(fractions, axis=(1, 2, 3))
    mass = fluid_state[0].reshape(zone_count).astype(jnp.bfloat16)
    selector = jnp.arange(listed, dtype=jnp.int32)[:, None] == slot_flat[None, :]
    weights = jnp.where(
        slot_flat[:, None] == jnp.arange(listed, dtype=jnp.int32)[None, :],
        mass[:, None], jnp.zeros((), jnp.bfloat16))
    flat_harm, partial_value = flat_and_moments(
        harmonics.reshape(harm_count, width_x * width_y, width_z), weights)
    block = round_up(-(-harm_count // device_count), 8)
    outer = device_count // INNER
    me = lax.axis_index("bricks")
    own_block = lax.rem(me, INNER) * outer + me // INNER
    padded_count = block * device_count
    spare = max(padded_count - partial_value.shape[0], 0)
    parts = jnp.pad(partial_value, ((0, spare), (0, 0)))[:padded_count].reshape(
        INNER, outer, block, listed
    )
    species = local_low.shape[0]
    extreme_row = jnp.pad(jnp.concatenate([-local_low, local_high]), (0, listed - 2 * species))
    small = jnp.pad(
        jnp.stack([my_bins.astype(jnp.float32), extreme_row]), ((0, 6), (0, 0))
    )
    own_degree = lax.dynamic_slice_in_dim(
        jnp.pad(degrees(harm_count), (0, padded_count - harm_count)), own_block * block, block)
    step_in, step_out, last_row = log_steps(shell_radius)
    first = jnp.arange(NB, dtype=jnp.int32) == 0
    grow_in = jnp.where(first[None, :], 0.0, jnp.exp((own_degree[:, None] + 1.0) * step_in[None, :]))
    grow_out = jnp.where(last_row[None, :], 0.0, jnp.exp(own_degree[:, None] * step_out[None, :]))
    radius = shell_radius[None, :]
    shells, extremes, halo = exchange(parts, small, grow_in, grow_out, radius, edges)
    halo = halo[:, :line_count].reshape(2, channels + 1, 1, width_y, width_z)
    below = jnp.where(me > 0, halo[0], jnp.zeros_like(halo[0]))
    beyond = jnp.where(me < device_count - 1, halo[1], jnp.zeros_like(halo[1]))
    padded = jnp.concatenate([below, rounded, beyond], axis=1).astype(extended.dtype)
    lower_bound = -extremes[1, :species]
    upper_bound = extremes[1, species : 2 * species]
    shell_mine = shells[:, :, :block].reshape(padded_count, listed)[:harm_count].T
    product = jnp.dot(shell_mine, flat_harm, preferred_element_type=jnp.float32)
    factor = -1.0 / math.sqrt(float(HARM * zone_count * device_count))
    potential = (jnp.sum(jnp.where(selector, product, 0.0), axis=0) * factor).reshape(
        width_x, width_y, width_z
    )
    potential_padded = padded_2(potential, (("bricks", 0),), 1)
    new_state = advance(fluid_state, padded, potential_padded, lower_bound, upper_bound)
    return (new_state, potential)


def solution(mesh):
    placed = (
        P(None, "bricks", None, None),
        P(None, "bricks", None, None),
        P("bricks", None, None),
        P("bricks", None),
        P(),
    )
    return jax.shard_map(
        per_device,
        mesh=mesh,
        in_specs=placed,
        out_specs=(P(None, "bricks", None, None), P("bricks", None, None)),
        check_vma=False,
    )
```

```python
import functools
import math

import jax
import jax.numpy as jnp
from jax import lax
from jax.experimental import pallas as pl
from jax.experimental.pallas import tpu as pltpu
from jax.sharding import PartitionSpec as P

LMAX = 40
HARM = 1681
NB = 1024


MESH = pl.DeviceIdType.MESH

time_step = 0.05


def padded_2(cells, sides, width):
    for axis, dim in sides:
        count = lax.axis_size(axis)
        ends = count - 1
        head = lax.slice_in_dim(cells, 0, width, axis=dim)
        tail = lax.slice_in_dim(cells, cells.shape[dim] - width, cells.shape[dim], axis=dim)
        cells = jnp.concatenate(
            [
                lax.ppermute(tail, axis, [(i, (i + 1) % count) for i in range(ends)]),
                cells,
                lax.ppermute(head, axis, [((i + 1) % count, i) for i in range(ends)]),
            ],
            axis=dim,
        )
    return cells


def degrees(harm_count):
    numbers = jnp.arange(harm_count, dtype=jnp.int32)
    marks = jnp.arange(1, LMAX + 1, dtype=jnp.int32) ** 2
    return jnp.sum((numbers[:, None] >= marks[None, :]).astype(jnp.int32), axis=1).astype(
        jnp.float32
    )


def log_steps(radius):
    bin_count = radius.shape[0]
    step_in = jnp.concatenate(
        [jnp.zeros((1,), radius.dtype), jnp.log(radius[:-1]) - jnp.log(radius[1:])]
    )
    step_out = jnp.concatenate([step_in[1:], jnp.zeros((1,), radius.dtype)])
    last_row = jnp.arange(bin_count, dtype=jnp.int32) == bin_count - 1
    return (step_in, step_out, last_row)


def round_up(value, step):
    return -(-value // step) * step


def one_hot(bin_row, row_total, listed):
    rows = lax.broadcasted_iota(jnp.int32, (row_total, listed), 0)
    return jnp.where(rows == bin_row, 1.0, 0.0).astype(jnp.bfloat16)


INNER = 8


def exchange_kernel(
    outer, part_ref, small_ref, grow_in_ref, grow_out_ref, radius_ref, edge_ref,
    shell_ref, extreme_ref, halo_ref,
    got, smalls, marks, sum_out, sum_in, dense, sent_back, came_back, worst, halo,
    small_send, small_recv, part_send, part_recv, sum_send, sum_recv,
    worst_send, worst_recv, dense_send, dense_recv, back_send, back_recv,
    edge_send, edge_recv,
):
    me = lax.axis_index("bricks")
    place, layer = lax.rem(me, INNER), me // INNER
    block, listed = part_ref.shape[2:]
    rows = radius_ref.shape[1]
    back_rows = dense.shape[1]

    def beside(offset):
        return lax.rem(place + offset, INNER)

    def above(offset):
        return lax.rem(layer + offset, outer)

    def in_layer(spot):
        return (layer * INNER + spot,)

    def in_column(level):
        return (level * INNER + place,)

    barrier = pltpu.get_barrier_semaphore()

    def greet_layer(offset, carry):
        pl.semaphore_signal(
            barrier, inc=1, device_id=in_layer(beside(offset)), device_id_type=MESH)
        return carry

    def greet_column(offset, carry):
        pl.semaphore_signal(
            barrier, inc=1, device_id=in_column(above(offset)), device_id_type=MESH)
        return carry

    count = outer * INNER
    ring = ((lax.rem(me + count - 1, count),), (lax.rem(me + 1, count),))
    for neighbour in ring:
        pl.semaphore_signal(barrier, inc=1, device_id=neighbour, device_id_type=MESH)
    lax.fori_loop(1, INNER, greet_layer, 0)
    lax.fori_loop(1, outer, greet_column, 0)
    smalls[place] = small_ref[...]
    got[place] = part_ref[place]
    pl.semaphore_wait(barrier, INNER + outer)

    def small_copy(spot, slot):
        return pltpu.make_async_remote_copy(
            src_ref=small_ref, dst_ref=smalls.at[slot], send_sem=small_send.at[spot],
            recv_sem=small_recv.at[slot], device_id=in_layer(spot), device_id_type=MESH)

    def part_copy(spot, slot, level):
        return pltpu.make_async_remote_copy(
            src_ref=part_ref.at[spot, level], dst_ref=got.at[slot, level],
            send_sem=part_send.at[spot, level], recv_sem=part_recv.at[slot, level],
            device_id=in_layer(spot), device_id_type=MESH)

    def sum_copy(level, slot):
        return pltpu.make_async_remote_copy(
            src_ref=sum_out.at[level], dst_ref=sum_in.at[slot], send_sem=sum_send.at[level],
            recv_sem=sum_recv.at[slot], device_id=in_column(level), device_id_type=MESH)

    def worst_copy(level, slot):
        return pltpu.make_async_remote_copy(
            src_ref=worst.at[layer], dst_ref=worst.at[slot], send_sem=worst_send.at[level],
            recv_sem=worst_recv.at[slot], device_id=in_column(level), device_id_type=MESH)

    def dense_copy(level, slot):
        return pltpu.make_async_remote_copy(
            src_ref=dense.at[layer], dst_ref=dense.at[slot], send_sem=dense_send.at[level],
            recv_sem=dense_recv.at[slot], device_id=in_column(level), device_id_type=MESH)

    def back_copy(spot, slot, level):
        return pltpu.make_async_remote_copy(
            src_ref=sent_back.at[spot, level], dst_ref=came_back.at[slot, level],
            send_sem=back_send.at[spot, level], recv_sem=back_recv.at[slot, level],
            device_id=in_layer(spot), device_id_type=MESH)

    edges = [
        pltpu.make_async_remote_copy(
            src_ref=edge_ref.at[side], dst_ref=halo.at[1 - side], send_sem=edge_send.at[side],
            recv_sem=edge_recv.at[1 - side], device_id=ring[side], device_id_type=MESH)
        for side in range(2)
    ]

    def send_small(offset, carry):
        small_copy(beside(offset), place).start()
        return carry

    lax.fori_loop(1, INNER, send_small, 0)

    def send_chunk(turn, carry):
        def send(offset, carry):
            part_copy(beside(offset), place, above(turn)).start()
            return carry

        return lax.fori_loop(1, INNER, send, carry)

    lax.fori_loop(1, outer + 1, send_chunk, 0)

    for edge in edges:
        edge.start()

    def columns(spot):
        return pl.ds(pl.multiple_of(spot * listed, listed), listed)

    def mark(spot):
        marks[:, columns(spot)] = one_hot(smalls[spot, 0:1, :].astype(jnp.int32), rows, listed)

    mark(place)

    def mark_other(offset, carry):
        spot = beside(INNER - offset)
        small_copy(beside(offset), spot).wait_recv()
        mark(spot)
        return carry

    lax.fori_loop(1, INNER, mark_other, 0)
    worst[layer] = jnp.max(smalls[...], axis=0)

    def send_worst(offset, carry):
        worst_copy(above(offset), layer).start()
        return carry

    lax.fori_loop(1, outer, send_worst, 0)

    def add_chunk(turn, carry):
        level = above(turn)

        def arrive(offset, carry):
            part_copy(beside(offset), beside(INNER - offset), level).wait_recv()
            return carry

        lax.fori_loop(1, INNER, arrive, 0)
        halves = []
        for spot in range(INNER):
            values = got[spot, level]
            high = values.astype(jnp.bfloat16).astype(jnp.float32)
            gap = jnp.zeros((64 - block, listed), jnp.float32)
            halves.append(
                jnp.concatenate([high, gap, values - high, gap], axis=0).astype(jnp.bfloat16)
            )
        both = lax.dot_general(
            marks[...], jnp.concatenate(halves, axis=1),
            (((1,), (1,)), ((), ())), preferred_element_type=jnp.float32)
        sum_out[level] = (both + pltpu.roll(both, 64, 1)).T[0:block]

        @pl.when(turn < outer)
        def _():
            sum_copy(level, layer).start()

        return carry

    lax.fori_loop(1, outer + 1, add_chunk, 0)
    sum_in[layer] = sum_out[layer]

    def sum_arrives(offset, carry):
        sum_copy(above(offset), above(outer - offset)).wait_recv()
        return carry

    lax.fori_loop(1, outer, sum_arrives, 0)
    scaled = jnp.sum(sum_in[...], axis=0) / radius_ref[...]
    field = -scaled
    for grow_ref, backward in ((grow_in_ref, False), (grow_out_ref, True)):
        factor, value = grow_ref[...], scaled
        step = 1
        while step < rows:
            turn = rows - step if backward else step
            value = value + factor * pltpu.roll(value, turn, 1)
            factor = factor * pltpu.roll(factor, turn, 1)
            step *= 2
        field = field + value
    if back_rows > block:
        field = jnp.concatenate(
            [field, jnp.zeros((back_rows - block, rows), jnp.float32)], axis=0)
    dense[layer] = field.astype(jnp.bfloat16)

    def send_dense(offset, carry):
        dense_copy(above(offset), layer).start()
        return carry

    lax.fori_loop(1, outer, send_dense, 0)

    def select(spot, level):
        return jnp.dot(
            dense[level], marks[:, columns(spot)], preferred_element_type=jnp.float32
        ).astype(jnp.bfloat16)

    def give_back(turn, carry):
        level = above(outer - turn)

        @pl.when(turn > 0)
        def _():
            dense_copy(above(turn), level).wait_recv()

        def give(offset, carry):
            spot = beside(offset)
            sent_back[spot, level] = select(spot, level)
            back_copy(spot, place, level).start()
            return carry

        lax.fori_loop(1, INNER, give, 0)
        came_back[place, level] = select(place, level)
        return carry

    lax.fori_loop(0, outer, give_back, 0)

    def finish_column(offset, carry):
        level, origin = above(offset), above(outer - offset)
        sum_copy(level, layer).wait_send()
        worst_copy(level, layer).wait_send()
        dense_copy(level, layer).wait_send()
        worst_copy(level, origin).wait_recv()
        return carry

    lax.fori_loop(1, outer, finish_column, 0)
    extreme_ref[...] = jnp.max(worst[...], axis=0)

    def finish_layer(offset, carry):
        spot, origin = beside(offset), beside(INNER - offset)
        small_copy(spot, place).wait_send()

        def finish(level, carry):
            part_copy(spot, place, level).wait_send()
            back_copy(spot, place, level).wait_send()
            back_copy(spot, origin, level).wait_recv()
            return carry

        return lax.fori_loop(0, outer, finish, carry)

    lax.fori_loop(1, INNER, finish_layer, 0)
    shell_ref[...] = came_back[...]
    for edge in edges:
        edge.wait()
    halo_ref[...] = halo[...]


def exchange(parts, small, grow_in, grow_out, radius, edges):
    inner, outer, block, listed = parts.shape
    rows = radius.shape[1]
    back_rows = round_up(block, 16)
    whole = pl.BlockSpec(memory_space=pltpu.VMEM)
    dma = pltpu.SemaphoreType.DMA
    return pl.pallas_call(
        functools.partial(exchange_kernel, outer),
        out_shape=(
            jax.ShapeDtypeStruct((inner, outer, back_rows, listed), jnp.bfloat16),
            jax.ShapeDtypeStruct(small.shape, jnp.float32),
            jax.ShapeDtypeStruct(edges.shape, edges.dtype),
        ),
        in_specs=[whole] * 6,
        out_specs=(whole, whole, whole),
        scratch_shapes=[
            pltpu.VMEM(parts.shape, jnp.float32),
            pltpu.VMEM((inner,) + small.shape, jnp.float32),
            pltpu.VMEM((rows, inner * listed), jnp.bfloat16),
            pltpu.VMEM((outer, block, rows), jnp.float32),
            pltpu.VMEM((outer, block, rows), jnp.float32),
            pltpu.VMEM((outer, back_rows, rows), jnp.bfloat16),
            pltpu.VMEM((inner, outer, back_rows, listed), jnp.bfloat16),
            pltpu.VMEM((inner, outer, back_rows, listed), jnp.bfloat16),
            pltpu.VMEM((outer,) + small.shape, jnp.float32),
            pltpu.VMEM(edges.shape, edges.dtype),
            dma((inner,)), dma((inner,)), dma((inner, outer)), dma((inner, outer)),
            dma((outer,)), dma((outer,)), dma((outer,)), dma((outer,)),
            dma((outer,)), dma((outer,)), dma((inner, outer)), dma((inner, outer)),
            dma((2,)), dma((2,)),
        ],
        compiler_params=pltpu.CompilerParams(
            collective_id=0, has_side_effects=True, vmem_limit_bytes=28 * 1024 * 1024
        ),
    )(parts, small, grow_in, grow_out, radius, edges)


TILE = 128


def moment_kernel(harm_count, harm_ref, weight_ref, flat_ref, part_ref):
    tile, lines, width = harm_ref.shape
    values = harm_ref[...].reshape(tile, lines * width)
    flat_ref[...] = values
    sums = jnp.dot(values, weight_ref[...], preferred_element_type=jnp.float32)
    number = pl.program_id(0) * tile + lax.broadcasted_iota(jnp.int32, sums.shape, 0)
    part_ref[...] = jnp.where(number < harm_count, sums, 0.0)


def flat_and_moments(harm, weights):
    harm_count, lines, width = harm.shape
    zone_count, listed = weights.shape
    steps = -(-harm_count // TILE)
    return pl.pallas_call(
        functools.partial(moment_kernel, harm_count),
        grid=(steps,),
        out_shape=(
            jax.ShapeDtypeStruct((harm_count, zone_count), harm.dtype),
            jax.ShapeDtypeStruct((steps * TILE, listed), jnp.float32),
        ),
        in_specs=[
            pl.BlockSpec((TILE, lines, width), lambda i: (i, 0, 0)),
            pl.BlockSpec((zone_count, listed), lambda i: (0, 0)),
        ],
        out_specs=(
            pl.BlockSpec((TILE, zone_count), lambda i: (i, 0)),
            pl.BlockSpec((TILE, listed), lambda i: (i, 0)),
        ),
        compiler_params=pltpu.CompilerParams(vmem_limit_bytes=28 * 1024 * 1024),
    )(harm, weights)


def advance(fluid_state, padded, potential_padded, lower_bound, upper_bound):
    channels = fluid_state.shape[0]
    speed = padded[channels]
    fields = padded[:channels]
    face_flux = 0.25 * (speed[1:] + speed[:-1])[None] * (fields[:, 1:] + fields[:, :-1])
    advanced = fluid_state - time_step * (face_flux[:, 1:] - face_flux[:, :-1])
    gradient = 0.5 * (potential_padded[2:] - potential_padded[:-2])
    density = advanced[0]
    momentum = advanced[1] - time_step * fluid_state[0] * gradient
    energy = advanced[4] - time_step * fluid_state[1] * gradient
    fraction = jnp.clip(
        advanced[5:] / density[None],
        lower_bound[:, None, None, None],
        upper_bound[:, None, None, None],
    )
    return jnp.concatenate(
        [density[None], momentum[None], advanced[2:4], energy[None], density[None] * fraction],
        axis=0,
    )


def per_device(fluid_state, harmonics, zone_slot, bin_list, shell_radius):
    channels, width_x, width_y, width_z = fluid_state.shape
    harm_count = harmonics.shape[0]
    zone_count = width_x * width_y * width_z
    device_count = lax.axis_size("bricks")
    slot_flat = zone_slot.reshape(zone_count)
    my_bins = bin_list[0]
    listed = my_bins.shape[0]
    velocity = fluid_state[1] / fluid_state[0]
    extended = jnp.concatenate([fluid_state, velocity[None]], axis=0)
    rounded = extended.astype(jnp.bfloat16)
    edges = jnp.stack([rounded[:, 0], rounded[:, -1]]).reshape(2, -1, width_z)
    line_count = edges.shape[1]
    edges = jnp.pad(edges, ((0, 0), (0, -line_count % 16), (0, 0)))
    fractions = fluid_state[5:] / fluid_state[0][None]
    local_low = jnp.min(fractions, axis=(1, 2, 3))
    local_high = jnp.max(fractions, axis=(1, 2, 3))
    mass = fluid_state[0].reshape(zone_count).astype(jnp.bfloat16)
    selector = jnp.arange(listed, dtype=jnp.int32)[:, None] == slot_flat[None, :]
    weights = jnp.where(
        slot_flat[:, None] == jnp.arange(listed, dtype=jnp.int32)[None, :],
        mass[:, None], jnp.zeros((), jnp.bfloat16))
    flat_harm, partial_value = flat_and_moments(
        harmonics.reshape(harm_count, width_x * width_y, width_z), weights)
    block = round_up(-(-harm_count // device_count), 8)
    outer = device_count // INNER
    me = lax.axis_index("bricks")
    own_block = lax.rem(me, INNER) * outer + me // INNER
    padded_count = block * device_count
    spare = max(padded_count - partial_value.shape[0], 0)
    parts = jnp.pad(partial_value, ((0, spare), (0, 0)))[:padded_count].reshape(
        INNER, outer, block, listed
    )
    species = local_low.shape[0]
    extreme_row = jnp.pad(jnp.concatenate([-local_low, local_high]), (0, listed - 2 * species))
    small = jnp.pad(
        jnp.stack([my_bins.astype(jnp.float32), extreme_row]), ((0, 6), (0, 0))
    )
    own_degree = lax.dynamic_slice_in_dim(
        jnp.pad(degrees(harm_count), (0, padded_count - harm_count)), own_block * block, block)
    step_in, step_out, last_row = log_steps(shell_radius)
    first = jnp.arange(NB, dtype=jnp.int32) == 0
    grow_in = jnp.where(first[None, :], 0.0, jnp.exp((own_degree[:, None] + 1.0) * step_in[None, :]))
    grow_out = jnp.where(last_row[None, :], 0.0, jnp.exp(own_degree[:, None] * step_out[None, :]))
    radius = shell_radius[None, :]
    shells, extremes, halo = exchange(parts, small, grow_in, grow_out, radius, edges)
    halo = halo[:, :line_count].reshape(2, channels + 1, 1, width_y, width_z)
    below = jnp.where(me > 0, halo[0], jnp.zeros_like(halo[0]))
    beyond = jnp.where(me < device_count - 1, halo[1], jnp.zeros_like(halo[1]))
    padded = jnp.concatenate([below, rounded, beyond], axis=1).astype(extended.dtype)
    lower_bound = -extremes[1, :species]
    upper_bound = extremes[1, species : 2 * species]
    shell_mine = shells[:, :, :block].reshape(padded_count, listed)[:harm_count].T
    product = jnp.dot(shell_mine, flat_harm, preferred_element_type=jnp.float32)
    factor = -1.0 / math.sqrt(float(HARM * zone_count * device_count))
    potential = (jnp.sum(jnp.where(selector, product, 0.0), axis=0) * factor).reshape(
        width_x, width_y, width_z
    )
    potential_padded = padded_2(potential, (("bricks", 0),), 1)
    new_state = advance(fluid_state, padded, potential_padded, lower_bound, upper_bound)
    return (new_state, potential)


def solution(mesh):
    placed = (
        P(None, "bricks", None, None),
        P(None, "bricks", None, None),
        P("bricks", None, None),
        P("bricks", None),
        P(),
    )
    return jax.shard_map(
        per_device,
        mesh=mesh,
        in_specs=placed,
        out_specs=(P(None, "bricks", None, None), P("bricks", None, None)),
        check_vma=False,
    )
```
